256 devices in a mesh: gy: 64 (over z, y, x_hi), gz: 4 (over x_lo, core).
Axes of the slice: x: 4 (x_hi: 2, x_lo: 2; x = x_hi * 2 + x_lo), y: 4, z: 8, core: 2. Of those that a mesh axis runs over, the one named last changes fastest.
Arguments:
- flow_state: bfloat16 [5, 4, 2048, 4096], P(None, 'gz', 'gy'), may hold values from -6 to 6
- mean_velocity: bfloat16 [2048, 4096], P('gy'), may hold values from 0.19921875 to 1.5
- mean_density: bfloat16 [2048, 4096], P('gy'), may hold values from 0.5 to 2
- mean_pressure: bfloat16 [2048, 4096], P('gy'), may hold values from 0.5 to 2
- deriv_x: bfloat16 [4096, 4096], P('gy', 'gz'), may hold values from -6 to 6
- deriv_y: bfloat16 [2048, 2048], replicated, may hold values from -6 to 6
Outputs:
- advanced: float32 [5, 4, 2048, 4096], P(None, 'gz', 'gy')
The draws below stay inside these ranges and needn't reach their ends.
All inputs are finite; a program needn't handle non-finite values.
Results may differ from the reference program's by a relative error of at most 0.0022.
Values may be sent and summed in bfloat16 or wider, within the bound.
A program may use at most 128 MiB of HBM per device.

```python
import math
import jax
import jax.numpy as jnp

NX = 4096
NY = 2048
FIELDS = 5
NZ = 4


def operator_table(key, matrix_order):
    first_key, second_key = jax.random.split(key)
    row_index = jnp.arange(matrix_order)[:, None].astype(jnp.float32)
    col_index = jnp.arange(matrix_order)[None, :].astype(jnp.float32)
    distance = jnp.abs(row_index - col_index)
    envelope = 0.6 * jnp.exp(-distance / 8.0) + 0.4 * matrix_order ** (-0.5)
    jitter = jnp.clip(jax.random.normal(first_key, (matrix_order, matrix_order), jnp.float32), -4.0, 4.0)
    metric = jnp.exp(jax.random.uniform(second_key, (1, matrix_order), jnp.float32, -0.7, 0.7))
    return (jitter * envelope * metric).astype(jnp.bfloat16)


def draw_deriv_x(key, part):
    return operator_table(jax.random.fold_in(key, 11), NX)


def draw_deriv_y(key, part):
    return operator_table(jax.random.fold_in(key, 23), NY)


def block_scale(key, extent, cuts, low, largest):
    gain = 1.0
    for dim, shards_of in cuts:
        heights = jax.random.uniform(jax.random.fold_in(jax.random.fold_in(key, 6), dim), (shards_of,), jnp.float32, low / len(cuts), largest / len(cuts))
        gain = gain * jnp.repeat(jnp.exp(heights), extent[dim] // shards_of).reshape((-1,) + (1,) * (len(extent) - 1 - dim))
    return gain


def centred(stream_key, dims, spread, reach, cuts=(), held_as=jnp.bfloat16):
    array = jax.random.normal(stream_key, dims, jnp.float32) * spread
    if len(cuts) > 0:
        array = block_scale(stream_key, dims, cuts, -0.22, 0.18) * array
    return jnp.clip(array, min=-reach, max=reach).astype(held_as)


def setup_inputs(seed: int = 0) -> dict:
    keys = jax.random.split(jax.random.key(seed), 7)
    flow_state = centred(keys[0], (FIELDS, NZ, NY, NX), 1.0, 6.0, ((1, 4), (2, 64)))
    mean_velocity = jnp.clip(0.19921875 + 1.3007812 * jax.random.uniform(keys[1], (NY, NX), jnp.float32) ** block_scale(keys[1], (NY, NX), ((0, 64),), -0.2, 0.2), 0.19921875, 1.5).astype(jnp.bfloat16)
    mean_density = jnp.clip(jnp.exp(math.log(2.0) - 1.3862944 * jax.random.uniform(keys[2], (NY, NX), jnp.float32) ** block_scale(keys[2], (NY, NX), ((0, 64),), -0.2, 0.2)), 0.5, 2.0).astype(jnp.bfloat16)
    mean_pressure = jnp.clip(jnp.exp(math.log(2.0) - 1.3862944 * jax.random.uniform(keys[3], (NY, NX), jnp.float32) ** block_scale(keys[3], (NY, NX), ((0, 64),), -0.2, 0.2)), 0.5, 2.0).astype(jnp.bfloat16)
    deriv_x = draw_deriv_x(jax.random.fold_in(keys[6], 71), 0)
    deriv_y = draw_deriv_y(jax.random.fold_in(keys[6], 71), 0)
    return dict(flow_state=flow_state, mean_velocity=mean_velocity, mean_density=mean_density, mean_pressure=mean_pressure, deriv_x=deriv_x, deriv_y=deriv_y)


def x_apply(fields_bf, deriv_x):
    layout = fields_bf.shape
    flattened = fields_bf.reshape(-1, layout[-1])
    product = jnp.dot(flattened, deriv_x, preferred_element_type=jnp.float32)
    return product.reshape(layout).astype(jnp.bfloat16)


def y_apply(two_fields, deriv_y):
    swapped = jnp.swapaxes(two_fields, 2, 3)
    layout = swapped.shape
    product = jnp.dot(swapped.reshape(-1, layout[-1]), deriv_y, preferred_element_type=jnp.float32)
    return jnp.swapaxes(product.reshape(layout), 2, 3).astype(jnp.bfloat16)


def z_apply(two_fields):
    above_plane = jnp.roll(two_fields, -1, axis=1).astype(jnp.float32)
    below_plane = jnp.roll(two_fields, 1, axis=1).astype(jnp.float32)
    return (above_plane - below_plane) * 1.5


def combine(along_x, along_y, along_z, mean_velocity, mean_density, mean_pressure):
    velocity = mean_velocity.astype(jnp.float32)
    density = mean_density.astype(jnp.float32)
    inverse = 1.0 / density
    stiffness = 1.4 * mean_pressure.astype(jnp.float32)
    slope_x = along_x.astype(jnp.float32)
    slope_y = along_y.astype(jnp.float32)
    divergence = slope_x[1] + slope_y[0] + along_z[0]
    return jnp.stack((
        -(velocity * slope_x[0] + density * divergence),
        -(velocity * slope_x[1] + inverse * slope_x[4]),
        -(velocity * slope_x[2] + inverse * slope_y[1]),
        -(velocity * slope_x[3] + inverse * along_z[1]),
        -(velocity * slope_x[4] + stiffness * divergence),
    ))


def reference(flow_state, mean_velocity, mean_density, mean_pressure, deriv_x, deriv_y):
    def rates_of(fields_bf):
        along_x = x_apply(fields_bf, deriv_x)
        along_y = y_apply(jnp.stack((fields_bf[2], fields_bf[4])), deriv_y)
        along_z = z_apply(jnp.stack((fields_bf[3], fields_bf[4])))
        return combine(along_x, along_y, along_z, mean_velocity, mean_density, mean_pressure)

    start_fields = flow_state.astype(jnp.float32)
    first = start_fields + 0.2 * rates_of(flow_state)
    first_half = first.astype(jnp.bfloat16)
    return 0.5 * (start_fields + first + 0.2 * rates_of(first_half))
```

```python
import jax
import jax.numpy as jnp
from jax import lax
from jax.experimental import pallas as pl
from jax.experimental.pallas import tpu as pltpu
from jax.sharding import PartitionSpec as P

MESH = pl.DeviceIdType.MESH
BF = jnp.bfloat16
F32 = jnp.float32
NA = 768
NB = 256
OFFS = (0, -1, 1, -2, 2, -3, 3, 4)


def kernel(
    flow, vel, rho, prs, dx, dy, out,
    DA, DB, DY, F1, F2, H1, H2, YG1, YG2, YT, YO1, YO2, B1, B2, A1, A2, R1, R2, S, VE, RH, PR, acc, sems,
):
    gy = lax.axis_index("gy")
    gz = lax.axis_index("gz")
    h = lax.rem(gy, 2)
    y = lax.rem(gy // 2, 4)
    z = gy // 8
    l = gz // 2
    c = lax.rem(gz, 2)

    count = [0]

    def new():
        count[0] += 1
        return count[0] - 1

    def zc(off):
        return lax.rem(z + (off + 8), 8)

    def yc(off):
        return lax.rem(y + (off + 4), 4)

    zdev = {d: (zc(d) * 8 + y * 2 + h, gz) for d in (1, -1)}
    ydev = {d: (z * 8 + yc(d) * 2 + h, gz) for d in (1, -1)}
    x2dev = (gy + 1 - 2 * h, gz)
    mate = (gy, gz + 1 - 2 * c)
    diag = (gy, 3 - gz)
    gyr = gy + l * (1 - 2 * h)
    gyl = gy + (1 - l) * (1 - 2 * h)
    right = {0: (gyr, (1 - l) * 2 + c), 1: (gyr, (1 - l) * 2 + 1 - c)}
    left = {0: (gyl, (1 - l) * 2 + c), 1: (gyl, (1 - l) * 2 + 1 - c)}

    def rc(src, dst, s, r, dev):
        return pltpu.make_async_remote_copy(
            src_ref=src, dst_ref=dst, send_sem=sems.at[s], recv_sem=sems.at[r], device_id=dev, device_id_type=MESH
        )

    def arrived(dst, r):
        rc(dst, dst, r, r, mate).wait_recv()

    def sent(src, s):
        rc(src, src, s, s, mate).wait_send()

    barrier = pltpu.get_barrier_semaphore()

    @pl.loop(1, 64)
    def _(k):
        pl.semaphore_signal(barrier, 1, device_id=(lax.rem(gy + k, 64), gz), device_id_type=MESH)

    for dev in (mate, right[0], right[1], left[0], left[1]):
        pl.semaphore_signal(barrier, 1, device_id=dev, device_id_type=MESH)

    base = gy * 64
    loads = {}
    for name, src, dst in (
        ("a", dx.at[:, pl.ds(0, NA)], DA.at[pl.ds(base, 64)]),
        ("b", dx.at[:, pl.ds(NA, NB)], DB.at[pl.ds(base, 64)]),
        ("f", flow, F1.at[0]),
        ("dy", dy, DY),
        ("v", vel, VE),
        ("r", rho, RH),
        ("p", prs, PR),
    ):
        loads[name] = pltpu.make_async_copy(src, dst, sems.at[new()])
        loads[name].start()

    pl.semaphore_wait(barrier, 68)

    sA, sB = new(), new()

    def rows(zz, yy, hh=None):
        b = (zz * 4 + yy) * 128
        if hh is None:
            return pl.ds(pl.multiple_of(b, 128), 128)
        return pl.ds(pl.multiple_of(b + hh * 64, 64), 64)

    def planes(zz, half=None):
        if half is None:
            return pl.ds(pl.multiple_of(zz * 512, 512), 512)
        return pl.ds(pl.multiple_of(zz * 512 + half * 256, 256), 256)

    def sendA(rs, dev, r):
        rc(DA.at[rs], DA.at[rs], sA, r, dev).start()

    def sendB(rs, dev, r):
        rc(DB.at[rs], DB.at[rs], sB, r, dev).start()

    hd = {1: 0, -1: 1}
    XA, XB = new(), new()
    Az = {(d, k): [new(), new()] if k == 1 else [new()] for d in (1, -1) for k in (1, 2, 3, 4)}
    Ay = {(i, d, k): [new(), new()] if (k == 1 and i == 0) else [new()] for i in range(8) for d in (1, -1) for k in (1, 2)}
    By = {(d, k): [new(), new()] if k == 1 else [new()] for d in (1, -1) for k in (1, 2)}
    Bz = {(d, k): new() for d in (1, -1) for k in (1, 2, 3, 4)}

    def first_hops(hh, piece):
        rs = rows(z, y, hh)
        for d in (1, -1):
            sendA(rs, zdev[d], Az[d, 1][piece])
            sendB(rs, ydev[d], By[d, 1][piece])
        for d in (1, -1):
            sendA(rs, ydev[d], Ay[0, d, 1][piece])

    def start_y(i):
        rs = rows(zc(OFFS[i]), y)
        for d in (1, -1):
            sendA(rs, ydev[d], Ay[i, d, 1][0])

    def on_az(d, k):
        zz = zc(-d * k)
        if k == 1:
            arrived(DA.at[rows(zz, y, 0)], Az[d, 1][0])
            arrived(DA.at[rows(zz, y, 1)], Az[d, 1][1])
        elif k < 4:
            arrived(DA.at[rows(zz, y)], Az[d, k][0])
        else:
            arrived(DA.at[rows(zz, y, hd[d])], Az[d, k][0])
        if k < 3:
            sendA(rows(zz, y), zdev[d], Az[d, k + 1][0])
        elif k == 3:
            sendA(rows(zz, y, hd[d]), zdev[d], Az[d, 4][0])
        if k < 4:
            start_y(OFFS.index(-d * k))
        elif d == -1:
            start_y(7)

    def on_ay1(i, d):
        zz, yy = zc(OFFS[i]), yc(-d)
        if i == 0:
            arrived(DA.at[rows(zz, yy, 0)], Ay[i, d, 1][0])
            arrived(DA.at[rows(zz, yy, 1)], Ay[i, d, 1][1])
        else:
            arrived(DA.at[rows(zz, yy)], Ay[i, d, 1][0])
        sendA(rows(zz, yy, hd[d]), ydev[d], Ay[i, d, 2][0])

    def on_ay2(i):
        for d in (1, -1):
            arrived(DA.at[rows(zc(OFFS[i]), yc(2), hd[d])], Ay[i, d, 2][0])
        step(DA, 0, NA // 256, zc(OFFS[i]), i == 0)

    def on_by1(d):
        arrived(DB.at[rows(z, yc(-d), 0)], By[d, 1][0])
        arrived(DB.at[rows(z, yc(-d), 1)], By[d, 1][1])
        sendB(rows(z, yc(-d), hd[d]), ydev[d], By[d, 2][0])

    def on_by2():
        for d in (1, -1):
            arrived(DB.at[rows(z, yc(2), hd[d])], By[d, 2][0])
        for d in (1, -1):
            sendB(planes(z), zdev[d], Bz[d, 1])

    def on_bz(d, k):
        zz = zc(-d * k)
        if k < 4:
            arrived(DB.at[planes(zz)], Bz[d, k])
        else:
            arrived(DB.at[planes(zz, hd[d])], Bz[d, k])
        if k < 3:
            sendB(planes(zz), zdev[d], Bz[d, k + 1])
        elif k == 3:
            sendB(planes(zz, hd[d]), zdev[d], Bz[d, 4])

    def step(D, col0, tiles, zz, first):
        ks = pl.ds(pl.multiple_of(zz * 512, 512), 512)

        @pl.loop(0, tiles)
        def _(n):
            cs = pl.ds(pl.multiple_of(n * 256, 256), 256)
            os = pl.ds(pl.multiple_of(col0 + n * 256, 256), 256)
            p = jnp.dot(F1[:, :, :, ks].reshape(640, 512), D[ks, cs], preferred_element_type=F32)
            if first:
                acc[:, os] = p
            else:
                acc[:, os] = acc[:, os] + p

    class Fields:
        pass

    def fields(F, H):
        q = Fields()
        q.F, q.H = F, H
        q.s, q.sh, q.rm, q.rl, q.rr, q.fl, q.fr, q.rh = [new() for _ in range(8)]
        return q

    LO, HI = pl.ds(0, 16), pl.ds(16, 16)

    def send_fields(q):
        F = q.F
        rc(F.at[0, :, HI], F.at[2, :, HI], q.s, q.rl, right[0]).start()
        rc(F.at[0, :, LO], F.at[2, :, LO], q.s, q.rr, left[0]).start()
        rc(F.at[0, pl.ds(3, 2)], q.H, q.sh, q.rh, diag).start()
        rc(F.at[0], F.at[1], q.s, q.rm, mate).start()

    def forward_fields(q):
        F = q.F
        arrived(F.at[2, :, HI], q.rl)
        rc(F.at[2, :, HI], F.at[3, :, HI], q.s, q.fl, mate).start()
        arrived(F.at[2, :, LO], q.rr)
        rc(F.at[2, :, LO], F.at[3, :, LO], q.s, q.fr, mate).start()

    def wait_forwarded(q):
        arrived(q.F.at[3, :, HI], q.fl)
        arrived(q.F.at[3, :, LO], q.fr)

    def finish_fields(q):
        sent(q.F.at[pl.ds(0, 3)], q.s)
        sent(q.F.at[0, pl.ds(3, 2)], q.sh)

    def lines(F, YG, YO, B):
        q = Fields()
        q.F, q.YG, q.YO, q.B = F, YG, YO, B
        q.s1, q.r1, q.l1, q.s2, q.r2, q.l2 = [new() for _ in range(6)]
        return q

    def unit(F, u):
        return F.at[0, 2 + 2 * (u // 32), :, pl.ds(pl.multiple_of(lax.rem(u, 32) * 128, 128), 128)]

    def block(k):
        return pl.ds(pl.multiple_of(k * 32, 32), 32)

    def send_lines(q):
        pltpu.make_async_copy(unit(q.F, gy), q.YG.at[block(gy)], sems.at[q.l1]).start()

        @pl.loop(1, 64)
        def _(k):
            u = lax.rem(gy + k, 64)
            rc(unit(q.F, u), q.YG.at[block(gy)], q.s1, q.r1, (u, gz)).start()

    def do_lines(q):
        pltpu.make_async_copy(unit(q.F, gy), q.YG.at[block(gy)], sems.at[q.l1]).wait()
        arrived(q.YG.at[pl.ds(0, 2016)], q.r1)

        @pl.loop(0, 8)
        def _(t):
            rs = pl.ds(pl.multiple_of(t * 256, 256), 256)
            YT[:, rs] = q.YG[rs, :].astype(F32).T.astype(BF)

        @pl.loop(0, 8)
        def _(t):
            rs = pl.ds(pl.multiple_of(t * 256, 256), 256)
            p = jnp.dot(YT[...], DY[:, rs], preferred_element_type=F32)
            q.YO[rs, :] = p.T.astype(BF)

        pltpu.make_async_copy(q.YO.at[block(gy)], q.B.at[gy], sems.at[q.l2]).start()

        @pl.loop(1, 64)
        def _(k):
            u = lax.rem(gy + k, 64)
            rc(q.YO.at[block(u)], q.B.at[gy], q.s2, q.r2, (u, gz)).start()

    def wait_lines(q):
        pltpu.make_async_copy(q.YO.at[block(gy)], q.B.at[gy], sems.at[q.l2]).wait()
        arrived(q.B.at[pl.ds(0, 63)], q.r2)

    def finish_lines(q):
        sent(q.YG.at[pl.ds(0, 2016)], q.s1)
        sent(q.YO.at[pl.ds(0, 2016)], q.s2)

    def results(A, R):
        q = Fields()
        q.A, q.R = A, R
        q.s, q.rm = new(), new()
        q.rr = [new(), new()]
        q.rl = [new(), new()]
        return q

    def send_mate(q):
        rc(q.R.at[0], q.A.at[gz], q.s, q.rm, mate).start()

    def send_sides(q):
        for o in (0, 1):
            rc(q.R.at[1 + o, :, HI], q.A.at[gz, :, HI], q.s, q.rr[o], left[o]).start()
            rc(q.R.at[1 + o, :, LO], q.A.at[gz, :, LO], q.s, q.rl[o], right[o]).start()

    def wait_results(q):
        arrived(q.A.at[mate[1]], q.rm)
        for o in (0, 1):
            arrived(q.A.at[right[o][1], :, HI], q.rr[o])
            arrived(q.A.at[left[o][1], :, LO], q.rl[o])

    def finish_results(q):
        sent(q.R, q.s)

    sgn = 1.5 - 3.0 * c.astype(F32)

    def rates(cb, qf, qy, qr):
        cs = pl.ds(pl.multiple_of(cb * 128, 128), 128)
        ls = pl.ds(pl.multiple_of(lax.rem(cb, 8) * 128, 128), 128)
        a = [qr.A[cb // 8, f, :, ls].astype(F32) for f in range(5)]
        b0 = qy.B[cb].astype(F32)
        b1 = qy.B[32 + cb].astype(F32)
        e0 = sgn * (qf.F[1, 3, :, cs].astype(F32) - qf.H[0, :, cs].astype(F32))
        e1 = sgn * (qf.F[1, 4, :, cs].astype(F32) - qf.H[1, :, cs].astype(F32))
        u = VE[:, cs].astype(F32)
        r = RH[:, cs].astype(F32)
        ib = 1.0 / r
        gp = 1.4 * PR[:, cs].astype(F32)
        div = a[1] + b0 + e0
        return cs, (
            -(u * a[0] + r * div),
            -(u * a[1] + ib * a[4]),
            -(u * a[2] + ib * b1),
            -(u * a[3] + ib * e1),
            -(u * a[4] + gp * div),
        )

    f1, f2 = fields(F1, H1), fields(F2, H2)
    y1, y2 = lines(F1, YG1, YO1, B1), lines(F2, YG2, YO2, B2)
    r1, r2 = results(A1, R1), results(A2, R2)

    loads["a"].wait()
    loads["b"].wait()
    own = rows(z, y, h)
    sendA(own, x2dev, XA)
    sendB(own, x2dev, XB)
    first_hops(h, 0)
    loads["f"].wait()
    send_fields(f1)
    other = rows(z, y, 1 - h)
    arrived(DA.at[other], XA)
    arrived(DB.at[other], XB)
    first_hops(1 - h, 1)
    send_lines(y1)

    def fields_in():
        forward_fields(f1)
        arrived(F1.at[1], f1.rm)
        wait_forwarded(f1)

    def lines_in():
        loads["dy"].wait()
        do_lines(y1)

    events = []
    for k in (1, 2, 3, 4):
        for d in (1, -1):
            events.append((5 + 6 * k, lambda d=d, k=k: on_az(d, k)))
            events.append((12 + 9 * k, lambda d=d, k=k: on_bz(d, k)))
    for d in (1, -1):
        events.append((9, lambda d=d: on_by1(d)))
    events.append((11.5, on_by2))
    for i in range(8):
        for d in (1, -1):
            events.append((10 + 6.5 * i, lambda i=i, d=d: on_ay1(i, d)))
        events.append((max(24.5, 15 + 6.5 * i), lambda i=i: on_ay2(i)))
    events.append((24, fields_in))
    events.append((30, lines_in))
    for i, o in enumerate(OFFS):
        events.append((max(24.6, 12.1 + 9 * abs(o)), lambda i=i, o=o: step(DB, NA, 1, zc(o), i == 0)))
    for _, act in sorted(events, key=lambda e: e[0]):
        act()

    @pl.loop(0, 4)
    def _(n):
        cs = pl.ds(pl.multiple_of(n * 256, 256), 256)
        v = acc[:, cs].astype(BF).reshape(4, 5, 32, 256)
        R1[:, :, :, cs] = v[1:]
        A1[gz, :, :, cs] = v[0]

    send_sides(r1)
    send_mate(r1)
    for name in ("v", "r", "p"):
        loads[name].wait()
    wait_lines(y1)
    arrived(H1, f1.rh)
    wait_results(r1)

    @pl.loop(0, 32)
    def _(cb):
        cs, rt = rates(cb, f1, y1, r1)
        for f in range(5):
            s0 = F1[0, f, :, cs].astype(F32)
            first = s0 + 0.2 * rt[f]
            F2[0, f, :, cs] = first.astype(BF)
            S[f, :, cs] = 0.5 * (s0 + first)

    send_fields(f2)
    send_lines(y2)

    def product(lo):
        for D, col0, tiles in ((DA, 0, NA // 256), (DB, NA, 1)):
            @pl.loop(0, tiles)
            def _(n):
                ds = pl.ds(pl.multiple_of(n * 256, 256), 256)
                cs = pl.ds(pl.multiple_of(col0 + n * 256, 256), 256)
                p = jnp.dot(F2[lo:lo + 2].reshape(320, 4096), D[:, ds], preferred_element_type=F32)
                v = p.astype(BF).reshape(2, 5, 32, 256)
                if lo == 0:
                    A2[gz, :, :, cs] = v[0]
                    R2[0, :, :, cs] = v[1]
                else:
                    R2[1:3, :, :, cs] = v

    arrived(F2.at[1], f2.rm)
    product(0)
    send_mate(r2)
    forward_fields(f2)
    wait_forwarded(f2)
    product(2)
    send_sides(r2)
    do_lines(y2)
    arrived(H2, f2.rh)
    wait_results(r2)
    wait_lines(y2)

    @pl.loop(0, 32)
    def _(cb):
        cs, rt = rates(cb, f2, y2, r2)
        for f in range(5):
            S[f, :, cs] = S[f, :, cs] + 0.1 * rt[f]

    store = pltpu.make_async_copy(S, out, sems.at[new()])
    store.start()
    sent(DA.at[pl.ds(0, 4032)], sA)
    sent(DB.at[pl.ds(0, 4032)], sB)
    for q in (f1, f2):
        finish_fields(q)
    for q in (y1, y2):
        finish_lines(q)
    for q in (r1, r2):
        finish_results(q)
    store.wait()
    assert count[0] <= 160, count[0]


def body(flow_state, mean_velocity, mean_density, mean_pressure, deriv_x, deriv_y):
    V = pltpu.VMEM
    out = pl.pallas_call(
        kernel,
        out_shape=jax.ShapeDtypeStruct((5, 32, 4096), F32),
        in_specs=[pl.BlockSpec(memory_space=pl.ANY)] * 6,
        out_specs=pl.BlockSpec(memory_space=pl.ANY),
        scratch_shapes=[
            V((4096, NA), BF), V((4096, NB), BF), V((2048, 2048), BF),
            V((4, 5, 32, 4096), BF), V((4, 5, 32, 4096), BF),
            V((2, 32, 4096), BF), V((2, 32, 4096), BF),
            V((2048, 128), BF), V((2048, 128), BF), V((128, 2048), BF), V((2048, 128), BF), V((2048, 128), BF),
            V((64, 32, 128), BF), V((64, 32, 128), BF),
            V((4, 5, 32, 1024), BF), V((4, 5, 32, 1024), BF), V((3, 5, 32, 1024), BF), V((3, 5, 32, 1024), BF),
            V((5, 32, 4096), F32), V((32, 4096), BF), V((32, 4096), BF), V((32, 4096), BF),
            V((640, 1024), F32),
            pltpu.SemaphoreType.DMA((160,)),
        ],
        compiler_params=pltpu.CompilerParams(collective_id=0, has_side_effects=True, vmem_limit_bytes=62 << 20),
        name="two_sections",
    )(flow_state.reshape(5, 32, 4096), mean_velocity, mean_density, mean_pressure, deriv_x, deriv_y)
    return out.reshape(5, 1, 32, 4096)


def solution(mesh):
    placed = (
        P(None, "gz", "gy", None),
        P("gy", None),
        P("gy", None),
        P("gy", None),
        P("gy", "gz"),
        P(),
    )
    return jax.shard_map(
        body, mesh=mesh, in_specs=placed, out_specs=P(None, "gz", "gy", None), check_vma=False
    )
```

```python
import jax
import jax.numpy as jnp
from jax import lax
from jax.experimental import pallas as pl
from jax.experimental.pallas import tpu as pltpu
from jax.sharding import PartitionSpec as P

MESH = pl.DeviceIdType.MESH
BF = jnp.bfloat16
F32 = jnp.float32
NA = 768
NB = 256
OFFS = (0, -1, 1, -2, 2, -3, 3, 4)
ORDER = (
    ("by", 1), ("by", -1), ("az", 1, 1), ("az", -1, 1), ("b2",), ("ay", 0, 1), ("ay", 0, -1),
    ("az", 1, 2), ("az", -1, 2), ("ay", 1, 1), ("ay", 1, -1), ("ay", 2, 1), ("ay", 2, -1), ("f",),
    ("bz", -1, 1), ("bz", 1, 1), ("as", 0), ("bs", 0), ("bs", 2), ("bs", 1),
    ("az", 1, 3), ("az", -1, 3), ("ay", 3, 1), ("ay", 3, -1), ("ay", 4, 1), ("ay", 4, -1), ("l",),
    ("bz", 1, 2), ("bz", -1, 2), ("az", 1, 4), ("az", -1, 4), ("as", 1), ("as", 2), ("bs", 3), ("bs", 4),
    ("as", 3), ("as", 4), ("bz", 1, 3), ("bz", -1, 3), ("ay", 5, 1), ("ay", 5, -1), ("ay", 6, 1), ("ay", 6, -1),
    ("bs", 5), ("bs", 6), ("bz", 1, 4), ("bz", -1, 4), ("ay", 7, 1), ("ay", 7, -1), ("bs", 7),
    ("as", 5), ("as", 6), ("as", 7),
)


def kernel(
    flow, vel, rho, prs, dx, dy, out,
    DA, DB, DY, F1, F2, H1, H2, YG1, YG2, YT, YO1, YO2, B1, B2, A1, A2, R1, R2, S, VE, RH, PR, acc, sems,
):
    gy = lax.axis_index("gy")
    gz = lax.axis_index("gz")
    h = lax.rem(gy, 2)
    y = lax.rem(gy // 2, 4)
    z = gy // 8
    l = gz // 2
    c = lax.rem(gz, 2)

    count = [0]

    def new():
        count[0] += 1
        return count[0] - 1

    def zc(off):
        return lax.rem(z + (off + 8), 8)

    def yc(off):
        return lax.rem(y + (off + 4), 4)

    zdev = {d: (zc(d) * 8 + y * 2 + h, gz) for d in (1, -1)}
    ydev = {d: (z * 8 + yc(d) * 2 + h, gz) for d in (1, -1)}
    x2dev = (gy + 1 - 2 * h, gz)
    mate = (gy, gz + 1 - 2 * c)
    diag = (gy, 3 - gz)
    gyr = gy + l * (1 - 2 * h)
    gyl = gy + (1 - l) * (1 - 2 * h)
    right = {0: (gyr, (1 - l) * 2 + c), 1: (gyr, (1 - l) * 2 + 1 - c)}
    left = {0: (gyl, (1 - l) * 2 + c), 1: (gyl, (1 - l) * 2 + 1 - c)}

    def rc(src, dst, s, r, dev):
        return pltpu.make_async_remote_copy(
            src_ref=src, dst_ref=dst, send_sem=sems.at[s], recv_sem=sems.at[r], device_id=dev, device_id_type=MESH
        )

    def arrived(dst, r):
        rc(dst, dst, r, r, mate).wait_recv()

    def sent(src, s):
        rc(src, src, s, s, mate).wait_send()

    barrier = pltpu.get_barrier_semaphore()

    @pl.loop(1, 64)
    def _(k):
        pl.semaphore_signal(barrier, 1, device_id=(lax.rem(gy + k, 64), gz), device_id_type=MESH)

    for dev in (mate, right[0], right[1], left[0], left[1]):
        pl.semaphore_signal(barrier, 1, device_id=dev, device_id_type=MESH)

    base = gy * 64
    loads = {}
    for name, src, dst in (
        ("a", dx.at[:, pl.ds(0, NA)], DA.at[pl.ds(base, 64)]),
        ("b", dx.at[:, pl.ds(NA, NB)], DB.at[pl.ds(base, 64)]),
        ("f", flow, F1.at[0]),
        ("dy", dy, DY),
        ("v", vel, VE),
        ("r", rho, RH),
        ("p", prs, PR),
    ):
        loads[name] = pltpu.make_async_copy(src, dst, sems.at[new()])
        loads[name].start()

    pl.semaphore_wait(barrier, 68)

    sA, sB = new(), new()

    def rows(zz, yy, hh=None):
        b = (zz * 4 + yy) * 128
        if hh is None:
            return pl.ds(pl.multiple_of(b, 128), 128)
        return pl.ds(pl.multiple_of(b + hh * 64, 64), 64)

    def planes(zz, half=None):
        if half is None:
            return pl.ds(pl.multiple_of(zz * 512, 512), 512)
        return pl.ds(pl.multiple_of(zz * 512 + half * 256, 256), 256)

    def sendA(rs, dev, r):
        rc(DA.at[rs], DA.at[rs], sA, r, dev).start()

    def sendB(rs, dev, r):
        rc(DB.at[rs], DB.at[rs], sB, r, dev).start()

    hd = {1: 0, -1: 1}
    XA, XB = new(), new()
    Az = {(d, k): [new(), new()] if k == 1 else [new()] for d in (1, -1) for k in (1, 2, 3, 4)}
    Ay = {(i, d, k): [new(), new()] if (k == 1 and i == 0) else [new()] for i in range(8) for d in (1, -1) for k in (1, 2)}
    By = {(d, k): [new(), new()] if k == 1 else [new()] for d in (1, -1) for k in (1, 2)}
    Bz = {(d, k): new() for d in (1, -1) for k in (1, 2, 3, 4)}

    def first_hops(hh, piece):
        rs = rows(z, y, hh)
        for d in (1, -1):
            sendA(rs, zdev[d], Az[d, 1][piece])
            sendB(rs, ydev[d], By[d, 1][piece])
        for d in (1, -1):
            sendA(rs, ydev[d], Ay[0, d, 1][piece])

    def start_y(i):
        rs = rows(zc(OFFS[i]), y)
        for d in (1, -1):
            sendA(rs, ydev[d], Ay[i, d, 1][0])

    def on_az(d, k):
        zz = zc(-d * k)
        if k == 1:
            arrived(DA.at[rows(zz, y, 0)], Az[d, 1][0])
            arrived(DA.at[rows(zz, y, 1)], Az[d, 1][1])
        elif k < 4:
            arrived(DA.at[rows(zz, y)], Az[d, k][0])
        else:
            arrived(DA.at[rows(zz, y, hd[d])], Az[d, k][0])
        if k < 3:
            sendA(rows(zz, y), zdev[d], Az[d, k + 1][0])
        elif k == 3:
            sendA(rows(zz, y, hd[d]), zdev[d], Az[d, 4][0])
        if k < 4:
            start_y(OFFS.index(-d * k))
        elif d == -1:
            start_y(7)

    def on_ay1(i, d):
        zz, yy = zc(OFFS[i]), yc(-d)
        if i == 0:
            arrived(DA.at[rows(zz, yy, 0)], Ay[i, d, 1][0])
            arrived(DA.at[rows(zz, yy, 1)], Ay[i, d, 1][1])
        else:
            arrived(DA.at[rows(zz, yy)], Ay[i, d, 1][0])
        sendA(rows(zz, yy, hd[d]), ydev[d], Ay[i, d, 2][0])

    def on_ay2(i):
        for d in (1, -1):
            arrived(DA.at[rows(zc(OFFS[i]), yc(2), hd[d])], Ay[i, d, 2][0])
        step(DA, 0, NA // 256, zc(OFFS[i]), i == 0)

    def on_by1(d):
        arrived(DB.at[rows(z, yc(-d), 0)], By[d, 1][0])
        arrived(DB.at[rows(z, yc(-d), 1)], By[d, 1][1])
        sendB(rows(z, yc(-d), hd[d]), ydev[d], By[d, 2][0])

    def on_by2():
        for d in (1, -1):
            arrived(DB.at[rows(z, yc(2), hd[d])], By[d, 2][0])
        for d in (1, -1):
            sendB(planes(z), zdev[d], Bz[d, 1])

    def on_bz(d, k):
        zz = zc(-d * k)
        if k < 4:
            arrived(DB.at[planes(zz)], Bz[d, k])
        else:
            arrived(DB.at[planes(zz, hd[d])], Bz[d, k])
        if k < 3:
            sendB(planes(zz), zdev[d], Bz[d, k + 1])
        elif k == 3:
            sendB(planes(zz, hd[d]), zdev[d], Bz[d, 4])

    def step(D, col0, tiles, zz, first):
        ks = pl.ds(pl.multiple_of(zz * 512, 512), 512)

        @pl.loop(0, tiles)
        def _(n):
            cs = pl.ds(pl.multiple_of(n * 256, 256), 256)
            os = pl.ds(pl.multiple_of(col0 + n * 256, 256), 256)
            p = jnp.dot(F1[:, :, :, ks].reshape(640, 512), D[ks, cs], preferred_element_type=F32)
            if first:
                acc[:, os] = p
            else:
                acc[:, os] = acc[:, os] + p

    class Fields:
        pass

    def fields(F, H):
        q = Fields()
        q.F, q.H = F, H
        q.s, q.sh, q.rm, q.rl, q.rr, q.fl, q.fr, q.rh = [new() for _ in range(8)]
        return q

    LO, HI = pl.ds(0, 16), pl.ds(16, 16)

    def send_fields(q):
        F = q.F
        rc(F.at[0, :, HI], F.at[2, :, HI], q.s, q.rl, right[0]).start()
        rc(F.at[0, :, LO], F.at[2, :, LO], q.s, q.rr, left[0]).start()
        rc(F.at[0, pl.ds(3, 2)], q.H, q.sh, q.rh, diag).start()
        rc(F.at[0], F.at[1], q.s, q.rm, mate).start()

    def forward_fields(q):
        F = q.F
        arrived(F.at[2, :, HI], q.rl)
        rc(F.at[2, :, HI], F.at[3, :, HI], q.s, q.fl, mate).start()
        arrived(F.at[2, :, LO], q.rr)
        rc(F.at[2, :, LO], F.at[3, :, LO], q.s, q.fr, mate).start()

    def wait_forwarded(q):
        arrived(q.F.at[3, :, HI], q.fl)
        arrived(q.F.at[3, :, LO], q.fr)

    def finish_fields(q):
        sent(q.F.at[pl.ds(0, 3)], q.s)
        sent(q.F.at[0, pl.ds(3, 2)], q.sh)

    def lines(F, YG, YO, B):
        q = Fields()
        q.F, q.YG, q.YO, q.B = F, YG, YO, B
        q.s1, q.r1, q.l1, q.s2, q.r2, q.l2 = [new() for _ in range(6)]
        return q

    def unit(F, u):
        return F.at[0, 2 + 2 * (u // 32), :, pl.ds(pl.multiple_of(lax.rem(u, 32) * 128, 128), 128)]

    def block(k):
        return pl.ds(pl.multiple_of(k * 32, 32), 32)

    def send_lines(q):
        pltpu.make_async_copy(unit(q.F, gy), q.YG.at[block(gy)], sems.at[q.l1]).start()

        @pl.loop(1, 64)
        def _(k):
            u = lax.rem(gy + k, 64)
            rc(unit(q.F, u), q.YG.at[block(gy)], q.s1, q.r1, (u, gz)).start()

    def do_lines(q):
        pltpu.make_async_copy(unit(q.F, gy), q.YG.at[block(gy)], sems.at[q.l1]).wait()
        arrived(q.YG.at[pl.ds(0, 2016)], q.r1)

        @pl.loop(0, 8)
        def _(t):
            rs = pl.ds(pl.multiple_of(t * 256, 256), 256)
            YT[:, rs] = q.YG[rs, :].astype(F32).T.astype(BF)

        @pl.loop(0, 8)
        def _(i):
            t = lax.rem(z + i, 8)
            rs = pl.ds(pl.multiple_of(t * 256, 256), 256)
            p = jnp.dot(YT[...], DY[:, rs], preferred_element_type=F32)
            q.YO[rs, :] = p.T.astype(BF)

            @pl.loop(0, 8)
            def _(k):
                u = t * 8 + lax.rem(gy + k, 8)

                @pl.when(u != gy)
                def _():
                    rc(q.YO.at[block(u)], q.B.at[gy], q.s2, q.r2, (u, gz)).start()

        pltpu.make_async_copy(q.YO.at[block(gy)], q.B.at[gy], sems.at[q.l2]).start()

    def wait_lines(q):
        pltpu.make_async_copy(q.YO.at[block(gy)], q.B.at[gy], sems.at[q.l2]).wait()
        arrived(q.B.at[pl.ds(0, 63)], q.r2)

    def finish_lines(q):
        sent(q.YG.at[pl.ds(0, 2016)], q.s1)
        sent(q.YO.at[pl.ds(0, 2016)], q.s2)

    def results(A, R):
        q = Fields()
        q.A, q.R = A, R
        q.s, q.rm = new(), new()
        q.rr = [new(), new()]
        q.rl = [new(), new()]
        return q

    def send_mate(q):
        rc(q.R.at[0], q.A.at[gz], q.s, q.rm, mate).start()

    def send_sides(q):
        for o in (0, 1):
            rc(q.R.at[1 + o, :, HI], q.A.at[gz, :, HI], q.s, q.rr[o], left[o]).start()
            rc(q.R.at[1 + o, :, LO], q.A.at[gz, :, LO], q.s, q.rl[o], right[o]).start()

    def wait_results(q):
        arrived(q.A.at[mate[1]], q.rm)
        for o in (0, 1):
            arrived(q.A.at[right[o][1], :, HI], q.rr[o])
            arrived(q.A.at[left[o][1], :, LO], q.rl[o])

    def finish_results(q):
        sent(q.R, q.s)

    sgn = 1.5 - 3.0 * c.astype(F32)

    def rates(cb, qf, qy, qr):
        cs = pl.ds(pl.multiple_of(cb * 128, 128), 128)
        ls = pl.ds(pl.multiple_of(lax.rem(cb, 8) * 128, 128), 128)
        a = [qr.A[cb // 8, f, :, ls].astype(F32) for f in range(5)]
        b0 = qy.B[cb].astype(F32)
        b1 = qy.B[32 + cb].astype(F32)
        e0 = sgn * (qf.F[1, 3, :, cs].astype(F32) - qf.H[0, :, cs].astype(F32))
        e1 = sgn * (qf.F[1, 4, :, cs].astype(F32) - qf.H[1, :, cs].astype(F32))
        u = VE[:, cs].astype(F32)
        r = RH[:, cs].astype(F32)
        ib = 1.0 / r
        gp = 1.4 * PR[:, cs].astype(F32)
        div = a[1] + b0 + e0
        return cs, (
            -(u * a[0] + r * div),
            -(u * a[1] + ib * a[4]),
            -(u * a[2] + ib * b1),
            -(u * a[3] + ib * e1),
            -(u * a[4] + gp * div),
        )

    f1, f2 = fields(F1, H1), fields(F2, H2)
    y1, y2 = lines(F1, YG1, YO1, B1), lines(F2, YG2, YO2, B2)
    r1, r2 = results(A1, R1), results(A2, R2)

    loads["a"].wait()
    loads["b"].wait()
    own = rows(z, y, h)
    sendA(own, x2dev, XA)
    sendB(own, x2dev, XB)
    first_hops(h, 0)
    loads["f"].wait()
    send_fields(f1)
    other = rows(z, y, 1 - h)
    arrived(DA.at[other], XA)
    arrived(DB.at[other], XB)
    first_hops(1 - h, 1)
    send_lines(y1)

    def fields_in():
        forward_fields(f1)
        arrived(F1.at[1], f1.rm)
        wait_forwarded(f1)

    def lines_in():
        loads["dy"].wait()
        do_lines(y1)

    acts = {"az": on_az, "ay": on_ay1, "as": on_ay2, "by": on_by1, "b2": on_by2, "bz": on_bz}
    acts["bs"] = lambda i: step(DB, NA, 1, zc(OFFS[i]), i == 0)
    acts["f"], acts["l"] = fields_in, lines_in
    for name, *where in ORDER:
        acts[name](*where)

    @pl.loop(0, 4)
    def _(n):
        cs = pl.ds(pl.multiple_of(n * 256, 256), 256)
        v = acc[:, cs].astype(BF).reshape(4, 5, 32, 256)
        R1[:, :, :, cs] = v[1:]
        A1[gz, :, :, cs] = v[0]

    send_sides(r1)
    send_mate(r1)
    for name in ("v", "r", "p"):
        loads[name].wait()
    wait_lines(y1)
    arrived(H1, f1.rh)
    wait_results(r1)

    @pl.loop(0, 32)
    def _(i):
        cb = lax.rem(gy + i, 32)
        cs, rt = rates(cb, f1, y1, r1)
        for f in range(5):
            s0 = F1[0, f, :, cs].astype(F32)
            first = s0 + 0.2 * rt[f]
            F2[0, f, :, cs] = first.astype(BF)
            S[f, :, cs] = 0.5 * (s0 + first)
        for o in (0, 32):
            u = cb + o

            @pl.when(u != gy)
            def _():
                rc(unit(F2, u), YG2.at[block(gy)], y2.s1, y2.r1, (u, gz)).start()

    pltpu.make_async_copy(unit(F2, gy), YG2.at[block(gy)], sems.at[y2.l1]).start()
    send_fields(f2)

    def product(lo):
        for D, col0, tiles in ((DA, 0, NA // 256), (DB, NA, 1)):
            @pl.loop(0, tiles)
            def _(n):
                ds = pl.ds(pl.multiple_of(n * 256, 256), 256)
                cs = pl.ds(pl.multiple_of(col0 + n * 256, 256), 256)
                p = jnp.dot(F2[lo:lo + 2].reshape(320, 4096), D[:, ds], preferred_element_type=F32)
                v = p.astype(BF).reshape(2, 5, 32, 256)
                if lo == 0:
                    A2[gz, :, :, cs] = v[0]
                    R2[0, :, :, cs] = v[1]
                else:
                    R2[1:3, :, :, cs] = v

    arrived(F2.at[1], f2.rm)
    product(0)
    send_mate(r2)
    forward_fields(f2)
    do_lines(y2)
    wait_forwarded(f2)
    product(2)
    send_sides(r2)
    arrived(H2, f2.rh)
    wait_results(r2)
    wait_lines(y2)

    @pl.loop(0, 32)
    def _(cb):
        cs, rt = rates(cb, f2, y2, r2)
        for f in range(5):
            S[f, :, cs] = S[f, :, cs] + 0.1 * rt[f]

    store = pltpu.make_async_copy(S, out, sems.at[new()])
    store.start()
    sent(DA.at[pl.ds(0, 4032)], sA)
    sent(DB.at[pl.ds(0, 4032)], sB)
    for q in (f1, f2):
        finish_fields(q)
    for q in (y1, y2):
        finish_lines(q)
    for q in (r1, r2):
        finish_results(q)
    store.wait()
    assert count[0] <= 160, count[0]


def body(flow_state, mean_velocity, mean_density, mean_pressure, deriv_x, deriv_y):
    V = pltpu.VMEM
    out = pl.pallas_call(
        kernel,
        out_shape=jax.ShapeDtypeStruct((5, 32, 4096), F32),
        in_specs=[pl.BlockSpec(memory_space=pl.ANY)] * 6,
        out_specs=pl.BlockSpec(memory_space=pl.ANY),
        scratch_shapes=[
            V((4096, NA), BF), V((4096, NB), BF), V((2048, 2048), BF),
            V((4, 5, 32, 4096), BF), V((4, 5, 32, 4096), BF),
            V((2, 32, 4096), BF), V((2, 32, 4096), BF),
            V((2048, 128), BF), V((2048, 128), BF), V((128, 2048), BF), V((2048, 128), BF), V((2048, 128), BF),
            V((64, 32, 128), BF), V((64, 32, 128), BF),
            V((4, 5, 32, 1024), BF), V((4, 5, 32, 1024), BF), V((3, 5, 32, 1024), BF), V((3, 5, 32, 1024), BF),
            V((5, 32, 4096), F32), V((32, 4096), BF), V((32, 4096), BF), V((32, 4096), BF),
            V((640, 1024), F32),
            pltpu.SemaphoreType.DMA((160,)),
        ],
        compiler_params=pltpu.CompilerParams(collective_id=0, has_side_effects=True, vmem_limit_bytes=62 << 20),
        name="two_sections",
    )(flow_state.reshape(5, 32, 4096), mean_velocity, mean_density, mean_pressure, deriv_x, deriv_y)
    return out.reshape(5, 1, 32, 4096)


def solution(mesh):
    placed = (
        P(None, "gz", "gy", None),
        P("gy", None),
        P("gy", None),
        P("gy", None),
        P("gy", "gz"),
        P(),
    )
    return jax.shard_map(
        body, mesh=mesh, in_specs=placed, out_specs=P(None, "gz", "gy", None), check_vma=False
    )
```

```python
import jax
import jax.numpy as jnp
from jax import lax
from jax.experimental import pallas as pl
from jax.experimental.pallas import tpu as pltpu
from jax.sharding import PartitionSpec as P

MESH = pl.DeviceIdType.MESH
BF = jnp.bfloat16
F32 = jnp.float32
NA = 768
NB = 256
OFFS = (0, -1, 1, -2, 2, -3, 3, 4)
ORDER = (
    ("by", 1), ("by", -1), ("az", 1, 1), ("az", -1, 1), ("b2",), ("ay", 0, 1), ("ay", 0, -1),
    ("az", 1, 2), ("az", -1, 2), ("ay", 1, 1), ("ay", 1, -1), ("ay", 2, 1), ("ay", 2, -1),
    ("bz", -1, 1), ("bz", 1, 1), ("f",), ("az", 1, 3), ("az", -1, 3), ("as", 0), ("bs", 0), ("bs", 2), ("bs", 1),
    ("ay", 3, 1), ("ay", 3, -1), ("ay", 4, 1), ("ay", 4, -1), ("l",),
    ("bz", 1, 2), ("bz", -1, 2), ("az", 1, 4), ("az", -1, 4), ("as", 1), ("as", 2), ("bs", 3), ("bs", 4),
    ("as", 3), ("as", 4), ("bz", 1, 3), ("bz", -1, 3), ("ay", 5, 1), ("ay", 5, -1), ("ay", 6, 1), ("ay", 6, -1),
    ("bs", 5), ("bs", 6), ("bz", 1, 4), ("bz", -1, 4), ("ay", 7, 1), ("ay", 7, -1), ("bs", 7),
    ("as", 5), ("as", 6), ("as", 7),
)


def kernel(
    flow, vel, rho, prs, dx, dy, out,
    DA, DB, DY, F1, F2, H1, H2, YG1, YG2, YT, YO1, YO2, B1, B2, A1, A2, R1, R2, S, VE, RH, PR, acc, sems,
):
    gy = lax.axis_index("gy")
    gz = lax.axis_index("gz")
    h = lax.rem(gy, 2)
    y = lax.rem(gy // 2, 4)
    z = gy // 8
    l = gz // 2
    c = lax.rem(gz, 2)

    count = [0]

    def new():
        count[0] += 1
        return count[0] - 1

    def zc(off):
        return lax.rem(z + (off + 8), 8)

    def yc(off):
        return lax.rem(y + (off + 4), 4)

    zdev = {d: (zc(d) * 8 + y * 2 + h, gz) for d in (1, -1)}
    ydev = {d: (z * 8 + yc(d) * 2 + h, gz) for d in (1, -1)}
    x2dev = (gy + 1 - 2 * h, gz)
    mate = (gy, gz + 1 - 2 * c)
    diag = (gy, 3 - gz)
    gyr = gy + l * (1 - 2 * h)
    gyl = gy + (1 - l) * (1 - 2 * h)
    right = {0: (gyr, (1 - l) * 2 + c), 1: (gyr, (1 - l) * 2 + 1 - c)}
    left = {0: (gyl, (1 - l) * 2 + c), 1: (gyl, (1 - l) * 2 + 1 - c)}

    def rc(src, dst, s, r, dev):
        return pltpu.make_async_remote_copy(
            src_ref=src, dst_ref=dst, send_sem=sems.at[s], recv_sem=sems.at[r], device_id=dev, device_id_type=MESH
        )

    def arrived(dst, r):
        rc(dst, dst, r, r, mate).wait_recv()

    def sent(src, s):
        rc(src, src, s, s, mate).wait_send()

    barrier = pltpu.get_barrier_semaphore()

    @pl.loop(1, 64)
    def _(k):
        pl.semaphore_signal(barrier, 1, device_id=(lax.rem(gy + k, 64), gz), device_id_type=MESH)

    for dev in (mate, right[0], right[1], left[0], left[1]):
        pl.semaphore_signal(barrier, 1, device_id=dev, device_id_type=MESH)

    base = gy * 64
    loads = {}
    for name, src, dst in (
        ("a", dx.at[:, pl.ds(0, NA)], DA.at[pl.ds(base, 64)]),
        ("b", dx.at[:, pl.ds(NA, NB)], DB.at[pl.ds(base, 64)]),
        ("f", flow, F1.at[0]),
        ("dy", dy, DY),
        ("v", vel, VE),
        ("r", rho, RH),
        ("p", prs, PR),
    ):
        loads[name] = pltpu.make_async_copy(src, dst, sems.at[new()])
        loads[name].start()

    pl.semaphore_wait(barrier, 68)

    sA, sB = new(), new()

    def rows(zz, yy, hh=None):
        b = (zz * 4 + yy) * 128
        if hh is None:
            return pl.ds(pl.multiple_of(b, 128), 128)
        return pl.ds(pl.multiple_of(b + hh * 64, 64), 64)

    def planes(zz, half=None):
        if half is None:
            return pl.ds(pl.multiple_of(zz * 512, 512), 512)
        return pl.ds(pl.multiple_of(zz * 512 + half * 256, 256), 256)

    def sendA(rs, dev, r):
        rc(DA.at[rs], DA.at[rs], sA, r, dev).start()

    def sendB(rs, dev, r):
        rc(DB.at[rs], DB.at[rs], sB, r, dev).start()

    hd = {1: 0, -1: 1}
    XA, XB = new(), new()
    Az = {(d, k): [new(), new()] if k == 1 else [new()] for d in (1, -1) for k in (1, 2, 3, 4)}
    Ay = {(i, d, k): [new(), new()] if (k == 1 and i == 0) else [new()] for i in range(8) for d in (1, -1) for k in (1, 2)}
    By = {(d, k): [new(), new()] if k == 1 else [new()] for d in (1, -1) for k in (1, 2)}
    Bz = {(d, k): new() for d in (1, -1) for k in (1, 2, 3, 4)}

    def first_hops(hh, piece):
        rs = rows(z, y, hh)
        for d in (1, -1):
            sendA(rs, zdev[d], Az[d, 1][piece])
            sendB(rs, ydev[d], By[d, 1][piece])
        for d in (1, -1):
            sendA(rs, ydev[d], Ay[0, d, 1][piece])

    def start_y(i):
        rs = rows(zc(OFFS[i]), y)
        for d in (1, -1):
            sendA(rs, ydev[d], Ay[i, d, 1][0])

    def on_az(d, k):
        zz = zc(-d * k)
        if k == 1:
            arrived(DA.at[rows(zz, y, 0)], Az[d, 1][0])
            arrived(DA.at[rows(zz, y, 1)], Az[d, 1][1])
        elif k < 4:
            arrived(DA.at[rows(zz, y)], Az[d, k][0])
        else:
            arrived(DA.at[rows(zz, y, hd[d])], Az[d, k][0])
        if k < 3:
            sendA(rows(zz, y), zdev[d], Az[d, k + 1][0])
        elif k == 3:
            sendA(rows(zz, y, hd[d]), zdev[d], Az[d, 4][0])
        if k < 4:
            start_y(OFFS.index(-d * k))
        elif d == -1:
            start_y(7)

    def on_ay1(i, d):
        zz, yy = zc(OFFS[i]), yc(-d)
        if i == 0:
            arrived(DA.at[rows(zz, yy, 0)], Ay[i, d, 1][0])
            arrived(DA.at[rows(zz, yy, 1)], Ay[i, d, 1][1])
        else:
            arrived(DA.at[rows(zz, yy)], Ay[i, d, 1][0])
        sendA(rows(zz, yy, hd[d]), ydev[d], Ay[i, d, 2][0])

    def on_ay2(i):
        for d in (1, -1):
            arrived(DA.at[rows(zc(OFFS[i]), yc(2), hd[d])], Ay[i, d, 2][0])
        step(DA, 0, NA // 256, zc(OFFS[i]), i == 0)

    def on_by1(d):
        arrived(DB.at[rows(z, yc(-d), 0)], By[d, 1][0])
        arrived(DB.at[rows(z, yc(-d), 1)], By[d, 1][1])
        sendB(rows(z, yc(-d), hd[d]), ydev[d], By[d, 2][0])

    def on_by2():
        for d in (1, -1):
            arrived(DB.at[rows(z, yc(2), hd[d])], By[d, 2][0])
        for d in (1, -1):
            sendB(planes(z), zdev[d], Bz[d, 1])

    def on_bz(d, k):
        zz = zc(-d * k)
        if k < 4:
            arrived(DB.at[planes(zz)], Bz[d, k])
        else:
            arrived(DB.at[planes(zz, hd[d])], Bz[d, k])
        if k < 3:
            sendB(planes(zz), zdev[d], Bz[d, k + 1])
        elif k == 3:
            sendB(planes(zz, hd[d]), zdev[d], Bz[d, 4])

    def step(D, col0, tiles, zz, first):
        ks = pl.ds(pl.multiple_of(zz * 512, 512), 512)

        @pl.loop(0, tiles)
        def _(n):
            cs = pl.ds(pl.multiple_of(n * 256, 256), 256)
            os = pl.ds(pl.multiple_of(col0 + n * 256, 256), 256)
            p = jnp.dot(F1[:, :, :, ks].reshape(640, 512), D[ks, cs], preferred_element_type=F32)
            if first:
                acc[:, os] = p
            else:
                acc[:, os] = acc[:, os] + p

    class Fields:
        pass

    def fields(F, H):
        q = Fields()
        q.F, q.H = F, H
        q.s, q.sh, q.rm, q.rl, q.rr, q.fl, q.fr, q.rh, q.lh = [new() for _ in range(9)]
        return q

    LO, HI = pl.ds(0, 16), pl.ds(16, 16)

    def send_fields(q):
        F = q.F
        rc(F.at[0, :, HI], F.at[2, :, HI], q.s, q.rl, right[0]).start()
        rc(F.at[0, :, LO], F.at[2, :, LO], q.s, q.rr, left[0]).start()
        rc(F.at[0], F.at[1], q.s, q.rm, mate).start()

    mine = pl.ds(pl.multiple_of(16 * l, 16), 16)
    theirs = pl.ds(pl.multiple_of(16 * (1 - l), 16), 16)

    def send_halo(q):
        rc(q.F.at[0, pl.ds(3, 2), mine], q.H.at[:, mine], q.sh, q.rh, diag).start()

    def near_halo(q):
        return pltpu.make_async_copy(q.F.at[3, pl.ds(3, 2), mine], q.H.at[:, mine], sems.at[q.lh])

    def wait_halo(q):
        near_halo(q).wait()
        arrived(q.H.at[:, theirs], q.rh)

    def forward_fields(q):
        F = q.F
        arrived(F.at[2, :, HI], q.rl)
        rc(F.at[2, :, HI], F.at[3, :, HI], q.s, q.fl, mate).start()
        arrived(F.at[2, :, LO], q.rr)
        rc(F.at[2, :, LO], F.at[3, :, LO], q.s, q.fr, mate).start()

    def wait_forwarded(q):
        arrived(q.F.at[3, :, HI], q.fl)
        arrived(q.F.at[3, :, LO], q.fr)

    def finish_fields(q):
        sent(q.F.at[pl.ds(0, 3)], q.s)
        sent(q.F.at[0, pl.ds(3, 2), mine], q.sh)

    def lines(F, YG, YO, B):
        q = Fields()
        q.F, q.YG, q.YO, q.B = F, YG, YO, B
        q.s1, q.r1, q.l1, q.s2, q.r2, q.l2 = [new() for _ in range(6)]
        return q

    def unit(F, u):
        return F.at[0, 2 + 2 * (u // 32), :, pl.ds(pl.multiple_of(lax.rem(u, 32) * 128, 128), 128)]

    def block(k):
        return pl.ds(pl.multiple_of(k * 32, 32), 32)

    def send_lines(q):
        pltpu.make_async_copy(unit(q.F, gy), q.YG.at[block(gy)], sems.at[q.l1]).start()

        @pl.loop(1, 64)
        def _(k):
            u = lax.rem(gy + k, 64)
            rc(unit(q.F, u), q.YG.at[block(gy)], q.s1, q.r1, (u, gz)).start()

    def do_lines(q):
        pltpu.make_async_copy(unit(q.F, gy), q.YG.at[block(gy)], sems.at[q.l1]).wait()
        arrived(q.YG.at[pl.ds(0, 2016)], q.r1)

        @pl.loop(0, 8)
        def _(t):
            rs = pl.ds(pl.multiple_of(t * 256, 256), 256)
            YT[:, rs] = q.YG[rs, :].astype(F32).T.astype(BF)

        @pl.loop(0, 8)
        def _(i):
            t = lax.rem(z + i, 8)
            rs = pl.ds(pl.multiple_of(t * 256, 256), 256)
            p = jnp.dot(YT[...], DY[:, rs], preferred_element_type=F32)
            q.YO[rs, :] = p.T.astype(BF)

            @pl.loop(0, 8)
            def _(k):
                u = t * 8 + lax.rem(gy + k, 8)

                @pl.when(u != gy)
                def _():
                    rc(q.YO.at[block(u)], q.B.at[gy], q.s2, q.r2, (u, gz)).start()

        pltpu.make_async_copy(q.YO.at[block(gy)], q.B.at[gy], sems.at[q.l2]).start()

    def wait_lines(q):
        pltpu.make_async_copy(q.YO.at[block(gy)], q.B.at[gy], sems.at[q.l2]).wait()
        arrived(q.B.at[pl.ds(0, 63)], q.r2)

    def finish_lines(q):
        sent(q.YG.at[pl.ds(0, 2016)], q.s1)
        sent(q.YO.at[pl.ds(0, 2016)], q.s2)

    def results(A, R):
        q = Fields()
        q.A, q.R = A, R
        q.s, q.rm = new(), new()
        q.rr = [new(), new()]
        q.rl = [new(), new()]
        return q

    def send_mate(q):
        rc(q.R.at[0], q.A.at[gz], q.s, q.rm, mate).start()

    def send_sides(q):
        for o in (0, 1):
            rc(q.R.at[1 + o, :, HI], q.A.at[gz, :, HI], q.s, q.rr[o], left[o]).start()
            rc(q.R.at[1 + o, :, LO], q.A.at[gz, :, LO], q.s, q.rl[o], right[o]).start()

    def wait_results(q):
        arrived(q.A.at[mate[1]], q.rm)
        for o in (0, 1):
            arrived(q.A.at[right[o][1], :, HI], q.rr[o])
            arrived(q.A.at[left[o][1], :, LO], q.rl[o])

    def finish_results(q):
        sent(q.R, q.s)

    sgn = 1.5 - 3.0 * c.astype(F32)

    def rates(cb, qf, qy, qr):
        cs = pl.ds(pl.multiple_of(cb * 128, 128), 128)
        ls = pl.ds(pl.multiple_of(lax.rem(cb, 8) * 128, 128), 128)
        a = [qr.A[cb // 8, f, :, ls].astype(F32) for f in range(5)]
        b0 = qy.B[cb].astype(F32)
        b1 = qy.B[32 + cb].astype(F32)
        e0 = sgn * (qf.F[1, 3, :, cs].astype(F32) - qf.H[0, :, cs].astype(F32))
        e1 = sgn * (qf.F[1, 4, :, cs].astype(F32) - qf.H[1, :, cs].astype(F32))
        u = VE[:, cs].astype(F32)
        r = RH[:, cs].astype(F32)
        ib = 1.0 / r
        gp = 1.4 * PR[:, cs].astype(F32)
        div = a[1] + b0 + e0
        return cs, (
            -(u * a[0] + r * div),
            -(u * a[1] + ib * a[4]),
            -(u * a[2] + ib * b1),
            -(u * a[3] + ib * e1),
            -(u * a[4] + gp * div),
        )

    f1, f2 = fields(F1, H1), fields(F2, H2)
    y1, y2 = lines(F1, YG1, YO1, B1), lines(F2, YG2, YO2, B2)
    r1, r2 = results(A1, R1), results(A2, R2)

    loads["a"].wait()
    loads["b"].wait()
    own = rows(z, y, h)
    sendA(own, x2dev, XA)
    sendB(own, x2dev, XB)
    first_hops(h, 0)
    loads["f"].wait()
    send_fields(f1)
    other = rows(z, y, 1 - h)
    arrived(DA.at[other], XA)
    arrived(DB.at[other], XB)
    first_hops(1 - h, 1)
    send_lines(y1)

    def fields_in():
        forward_fields(f1)
        send_halo(f1)
        arrived(F1.at[1], f1.rm)
        wait_forwarded(f1)
        near_halo(f1).start()

    def lines_in():
        loads["dy"].wait()
        do_lines(y1)

    acts = {"az": on_az, "ay": on_ay1, "as": on_ay2, "by": on_by1, "b2": on_by2, "bz": on_bz}
    acts["bs"] = lambda i: step(DB, NA, 1, zc(OFFS[i]), i == 0)
    acts["f"], acts["l"] = fields_in, lines_in
    for name, *where in ORDER:
        acts[name](*where)

    @pl.loop(0, 4)
    def _(n):
        cs = pl.ds(pl.multiple_of(n * 256, 256), 256)
        v = acc[:, cs].astype(BF).reshape(4, 5, 32, 256)
        R1[:, :, :, cs] = v[1:]
        A1[gz, :, :, cs] = v[0]

    send_sides(r1)
    send_mate(r1)
    for name in ("v", "r", "p"):
        loads[name].wait()
    wait_lines(y1)
    wait_halo(f1)
    wait_results(r1)

    @pl.loop(0, 32)
    def _(i):
        cb = lax.rem(gy + i, 32)
        cs, rt = rates(cb, f1, y1, r1)
        for f in range(5):
            s0 = F1[0, f, :, cs].astype(F32)
            first = s0 + 0.2 * rt[f]
            F2[0, f, :, cs] = first.astype(BF)
            S[f, :, cs] = 0.5 * (s0 + first)
        for o in (0, 32):
            u = cb + o

            @pl.when(u != gy)
            def _():
                rc(unit(F2, u), YG2.at[block(gy)], y2.s1, y2.r1, (u, gz)).start()

    pltpu.make_async_copy(unit(F2, gy), YG2.at[block(gy)], sems.at[y2.l1]).start()
    send_fields(f2)

    def product(lo):
        for D, col0, tiles in ((DA, 0, NA // 256), (DB, NA, 1)):
            @pl.loop(0, tiles)
            def _(n):
                ds = pl.ds(pl.multiple_of(n * 256, 256), 256)
                cs = pl.ds(pl.multiple_of(col0 + n * 256, 256), 256)
                p = jnp.dot(F2[lo:lo + 2].reshape(320, 4096), D[:, ds], preferred_element_type=F32)
                v = p.astype(BF).reshape(2, 5, 32, 256)
                if lo == 0:
                    A2[gz, :, :, cs] = v[0]
                    R2[0, :, :, cs] = v[1]
                else:
                    R2[1:3, :, :, cs] = v

    arrived(F2.at[1], f2.rm)
    product(0)
    send_mate(r2)
    forward_fields(f2)
    send_halo(f2)
    do_lines(y2)
    wait_forwarded(f2)
    near_halo(f2).start()
    product(2)
    send_sides(r2)
    wait_halo(f2)
    wait_results(r2)
    wait_lines(y2)

    stores = []
    for part in range(4):
        @pl.loop(part * 8, part * 8 + 8)
        def _(cb):
            cs, rt = rates(cb, f2, y2, r2)
            for f in range(5):
                S[f, :, cs] = S[f, :, cs] + 0.1 * rt[f]

        ps = pl.ds(part * 1024, 1024)
        stores.append(pltpu.make_async_copy(S.at[:, :, ps], out.at[:, :, ps], sems.at[new()]))
        stores[-1].start()
    sent(DA.at[pl.ds(0, 4032)], sA)
    sent(DB.at[pl.ds(0, 4032)], sB)
    for q in (f1, f2):
        finish_fields(q)
    for q in (y1, y2):
        finish_lines(q)
    for q in (r1, r2):
        finish_results(q)
    for store in stores:
        store.wait()
    assert count[0] <= 160


def body(flow_state, mean_velocity, mean_density, mean_pressure, deriv_x, deriv_y):
    V = pltpu.VMEM
    out = pl.pallas_call(
        kernel,
        out_shape=jax.ShapeDtypeStruct((5, 32, 4096), F32),
        in_specs=[pl.BlockSpec(memory_space=pl.ANY)] * 6,
        out_specs=pl.BlockSpec(memory_space=pl.ANY),
        scratch_shapes=[
            V((4096, NA), BF), V((4096, NB), BF), V((2048, 2048), BF),
            V((4, 5, 32, 4096), BF), V((4, 5, 32, 4096), BF),
            V((2, 32, 4096), BF), V((2, 32, 4096), BF),
            V((2048, 128), BF), V((2048, 128), BF), V((128, 2048), BF), V((2048, 128), BF), V((2048, 128), BF),
            V((64, 32, 128), BF), V((64, 32, 128), BF),
            V((4, 5, 32, 1024), BF), V((4, 5, 32, 1024), BF), V((3, 5, 32, 1024), BF), V((3, 5, 32, 1024), BF),
            V((5, 32, 4096), F32), V((32, 4096), BF), V((32, 4096), BF), V((32, 4096), BF),
            V((640, 1024), F32),
            pltpu.SemaphoreType.DMA((160,)),
        ],
        compiler_params=pltpu.CompilerParams(collective_id=0, has_side_effects=True, vmem_limit_bytes=62 << 20),
        name="two_sections",
    )(flow_state.reshape(5, 32, 4096), mean_velocity, mean_density, mean_pressure, deriv_x, deriv_y)
    return out.reshape(5, 1, 32, 4096)


def solution(mesh):
    placed = (
        P(None, "gz", "gy", None),
        P("gy", None),
        P("gy", None),
        P("gy", None),
        P("gy", "gz"),
        P(),
    )
    return jax.shard_map(
        body, mesh=mesh, in_specs=placed, out_specs=P(None, "gz", "gy", None), check_vma=False
    )
```
